512 devices in a mesh: dp: 16 (over z, core), seq: 32 (over y, x).
Axes of the slice: x: 4, y: 8, z: 8, core: 2. Of those that a mesh axis runs over, the one named last changes fastest.
Arguments:
- queries: bfloat16 [16, 4096, 2048], P('dp', 'seq'), may hold values from -110 to 110
- keys: bfloat16 [16, 4096, 512], P('dp', 'seq'), may hold values from -6 to 6
- values: bfloat16 [16, 4096, 512], P('dp', 'seq'), may hold values from -6 to 6
- grad_out: bfloat16 [16, 4096, 2048], P('dp', 'seq'), may hold values from -6 to 6
- doc_ids: int32 [16, 4096], P('dp'), may hold values from 0 to 15, never falling along the last dimension, each value on 1 to 2048 neighbouring positions
- partner_bits: int32 [16, 32], P('dp'), may hold values from 0 to 31
- q_gain: float32 [16, 128], replicated, may hold values from 0.5 to 1.5
Outputs:
- grad_queries: bfloat16 [16, 4096, 2048], P('dp', 'seq')
- grad_keys: bfloat16 [16, 4096, 512], P('dp', 'seq')
- grad_values: bfloat16 [16, 4096, 512], P('dp', 'seq')
- grad_gain: float32 [16, 128], replicated
The draws below stay inside these ranges and needn't reach their ends.
All inputs are finite; a program needn't handle non-finite values.
Results may differ from the reference program's by a relative error of at most 0.01.
Values may be sent and summed in bfloat16 or wider, within the bound.
No kernel may reach another device: no remote copies, remote signals or barrier semaphores. Data moves between devices by JAX's collectives and lax.ppermute only.
A program may use at most 64 MiB of HBM per device.

```python
import math
import jax
import jax.numpy as jnp
import numpy as np
from jax import lax

HEADS = 16
KV_HEADS = 4
HEAD_DIM = 128
BLOCK = 128
LEVELS = 5
SEQLEN = 4096
SEQS = 16
N_SEQ = 32


def shared_keys(key):
    base = jax.random.normal(key, (SEQS, SEQLEN, KV_HEADS * HEAD_DIM), jnp.float32)
    return jnp.clip(base, -6.0, 6.0)


def draw_keys(key, part):
    base = shared_keys(key)
    return base.astype(jnp.bfloat16)


def draw_queries(key, part):
    key = jax.random.fold_in(key, 5)
    own_key = jax.random.fold_in(key, 0)
    fresh = jnp.clip(jax.random.normal(own_key, (SEQS, SEQLEN, HEADS * HEAD_DIM), jnp.float32), -6.0, 6.0)
    return fresh.astype(jnp.bfloat16)


def with_ends(entries, stream_key, least, top_value):
    spot = [jax.random.randint(jax.random.fold_in(stream_key, axis), (), 0, length) for axis, length in enumerate(entries.shape)]
    main_axis = entries.shape.index(max(entries.shape))
    neighbour = spot[:main_axis] + [(spot[main_axis] + 1) % entries.shape[main_axis]] + spot[main_axis + 1:]
    return entries.at[tuple(spot)].set(least).at[tuple(neighbour)].set(top_value)


def levels(rng, extent, cuts, low, largest):
    def one(dim, parts):
        steps = jax.random.uniform(jax.random.fold_in(jax.random.fold_in(rng, 6), dim), (parts,), jnp.float32, low / len(cuts), largest / len(cuts))
        return jnp.repeat(jnp.exp(steps), extent[dim] // parts).reshape((-1,) + (1,) * (len(extent) - dim - 1))

    gain = one(*cuts[0])
    for cut in cuts[1:]:
        gain = gain * one(*cut)
    return gain


def length_profile(amount, total, reach, skew):
    loads = [(1 << 20) // math.isqrt(standing ** skew) + 1 for standing in range(2, amount + 1)]
    spare, counts = total - reach - (amount - 1), [1] * (amount - 1)
    while spare > 0:
        free = [i for i in range(amount - 1) if counts[i] < reach]
        whole, budget = sum([loads[i] for i in free]), spare
        for i in free:
            addition = min(reach - counts[i], max(1, budget * loads[i] // whole), spare)
            counts[i] = counts[i] + addition
            spare = spare - addition
    return np.array([reach] + counts)


def uneven_parts(key, count, total, reach, lean):
    if count == 2:
        one = jax.random.randint(key, (), max(1, total - reach), min(reach, total - 1) + 1)
        return jnp.stack([one, total - one])
    lengths = jnp.asarray(length_profile(count, total, reach, lean), jnp.int32)
    twos = (count - 1) // 2
    giver, taker = lengths[1:1 + 2 * twos:2], lengths[2:2 + 2 * twos:2]
    margin = jnp.minimum(giver - 1, reach - taker)
    shifted = jax.random.randint(jax.random.fold_in(key, 1), (twos,), 0, 1 << 20) % (margin + 1)
    lengths = lengths.at[1:1 + 2 * twos:2].set(giver - shifted).at[2:2 + 2 * twos:2].set(taker + shifted)
    return lengths[jax.random.permutation(jax.random.fold_in(key, 2), count)]


def scatter_about(rng, shape, spread, limit, pieces=(), kind=jnp.bfloat16):
    entries = spread * jax.random.normal(rng, shape, jnp.float32)
    if pieces:
        entries = entries * levels(rng, shape, pieces, -0.22, 0.18)
    return jnp.clip(entries, -limit, limit).astype(kind)


def setup_inputs(seed: int = 0) -> dict:
    streams_of = jax.random.split(jax.random.key(seed), 8)
    return {
        "queries": draw_queries(jax.random.fold_in(streams_of[7], 71), 0),
        "keys": draw_keys(jax.random.fold_in(streams_of[7], 71), 0),
        "values": scatter_about(streams_of[2], (SEQS, SEQLEN, KV_HEADS * HEAD_DIM), 1.0, 6.0, ((0, 16), (1, 32))),
        "grad_out": scatter_about(streams_of[3], (SEQS, SEQLEN, HEADS * HEAD_DIM), 1.0, 6.0, ((0, 16), (1, 32))),
        "doc_ids": jax.vmap(lambda own: jnp.searchsorted(jnp.cumsum(uneven_parts(own, N_SEQ // 2, SEQLEN, SEQLEN // 2, 2)), jnp.arange(SEQLEN), side="right"))(jax.random.split(streams_of[4], SEQS)).reshape((SEQS, SEQLEN)).astype(jnp.int32),
        "partner_bits": with_ends(jax.random.randint(streams_of[5], (SEQS, N_SEQ), 0, N_SEQ), jax.random.fold_in(streams_of[5], 1), 0, N_SEQ - 1).astype(jnp.int32),
        "q_gain": jnp.clip(1.0 + 0.1 * jax.random.normal(streams_of[6], (HEADS, HEAD_DIM), jnp.float32), 0.5, 1.5),
    }


def attend_block(q_group, out_grad, key_group, value_group, mask, scale):
    qf = q_group.astype(jnp.float32)
    gf = out_grad.astype(jnp.float32)
    kf = key_group.astype(jnp.float32)
    vf = value_group.astype(jnp.float32)
    scores = jnp.einsum('brd,kd->rbk', qf, kf) * scale
    scores = jnp.where(mask[None], scores, jnp.float32(-1e30))
    top = jnp.max(scores, axis=-1, keepdims=True)
    expo = jnp.exp(scores - top)
    total = jnp.sum(expo, axis=-1, keepdims=True)
    prob = expo / total
    prob_half = prob.astype(jnp.bfloat16)
    output = jnp.einsum('rbk,kd->brd', prob_half.astype(jnp.float32), vf).astype(jnp.bfloat16)
    delta = jnp.sum(gf * output.astype(jnp.float32), axis=-1).T
    dprob = jnp.einsum('brd,kd->rbk', gf, vf)
    dscore = (prob * (dprob - delta[:, :, None])).astype(jnp.bfloat16)
    dsf = dscore.astype(jnp.float32)
    dquery = jnp.einsum('rbk,kd->brd', dsf, kf) * scale
    dkey = jnp.einsum('rbk,brd->kd', dsf, qf) * scale
    dvalue = jnp.einsum('rbk,brd->kd', prob_half.astype(jnp.float32), gf)
    return dquery, dkey, dvalue


def reference(queries, keys, values, grad_out, doc_ids, partner_bits, q_gain):
    scale = HEAD_DIM ** -0.5
    group = HEADS // KV_HEADS
    offsets = jnp.arange(BLOCK, dtype=jnp.int32)

    def one_sequence(items):
        query, key, value, grad, docs, bits = items
        raw = query.reshape(SEQLEN, HEADS, HEAD_DIM)
        scaled = (raw.astype(jnp.float32) * q_gain).astype(jnp.bfloat16)
        dout = grad.reshape(SEQLEN, HEADS, HEAD_DIM)

        def step(carry, index):
            key_acc, value_acc, gain_acc = carry
            start = (index * BLOCK).astype(jnp.int32)
            q_blk = lax.dynamic_slice_in_dim(scaled, start, BLOCK, 0)
            raw_blk = lax.dynamic_slice_in_dim(raw, start, BLOCK, 0)
            g_blk = lax.dynamic_slice_in_dim(dout, start, BLOCK, 0)
            q_docs = lax.dynamic_slice_in_dim(docs, start, BLOCK, 0)
            q_pos = start + offsets
            my_bits = bits[index]
            starts = []
            key_rows = []
            value_rows = []
            masks = []
            for level in range(LEVELS + 1):
                if level == 0:
                    source = index
                    live = jnp.bool_(True)
                else:
                    dist = 2 ** (level - 1)
                    source = index - dist
                    live = ((my_bits // dist) % 2 == 1) & (index >= dist)
                first = (jnp.maximum(source, 0) * BLOCK).astype(jnp.int32)
                starts.append(first)
                key_rows.append(lax.dynamic_slice_in_dim(key, first, BLOCK, 0))
                value_rows.append(lax.dynamic_slice_in_dim(value, first, BLOCK, 0))
                k_docs = lax.dynamic_slice_in_dim(docs, first, BLOCK, 0)
                k_pos = first + offsets
                masks.append(live & (k_docs[None, :] == q_docs[:, None]) & (k_pos[None, :] <= q_pos[:, None]))
            all_keys = jnp.concatenate(key_rows, 0).reshape(-1, KV_HEADS, HEAD_DIM)
            all_values = jnp.concatenate(value_rows, 0).reshape(-1, KV_HEADS, HEAD_DIM)
            mask = jnp.concatenate(masks, 1)
            dq_parts = []
            dk_parts = []
            dv_parts = []
            for head in range(KV_HEADS):
                lo = head * group
                dquery, dkey, dvalue = attend_block(q_blk[:, lo:lo + group], g_blk[:, lo:lo + group],
                                                    all_keys[:, head], all_values[:, head], mask, scale)
                dq_parts.append(dquery)
                dk_parts.append(dkey)
                dv_parts.append(dvalue)
            dquery = jnp.concatenate(dq_parts, 1)
            key_grad = jnp.stack(dk_parts, 1).reshape(-1, KV_HEADS * HEAD_DIM)
            value_grad = jnp.stack(dv_parts, 1).reshape(-1, KV_HEADS * HEAD_DIM)
            for level in range(LEVELS + 1):
                first = starts[level]
                piece_k = key_grad[level * BLOCK:(level + 1) * BLOCK]
                piece_v = value_grad[level * BLOCK:(level + 1) * BLOCK]
                if level > 0:
                    piece_k = lax.optimization_barrier(piece_k.astype(jnp.bfloat16)).astype(jnp.float32)
                    piece_v = lax.optimization_barrier(piece_v.astype(jnp.bfloat16)).astype(jnp.float32)
                old_k = lax.dynamic_slice_in_dim(key_acc, first, BLOCK, 0)
                old_v = lax.dynamic_slice_in_dim(value_acc, first, BLOCK, 0)
                key_acc = lax.dynamic_update_slice_in_dim(key_acc, old_k + piece_k, first, 0)
                value_acc = lax.dynamic_update_slice_in_dim(value_acc, old_v + piece_v, first, 0)
            gain_acc = gain_acc + jnp.sum(dquery * raw_blk.astype(jnp.float32), axis=0)
            dq_blk = (dquery * q_gain).astype(jnp.bfloat16).reshape(BLOCK, HEADS * HEAD_DIM)
            return (key_acc, value_acc, gain_acc), dq_blk

        init = (jnp.zeros((SEQLEN, KV_HEADS * HEAD_DIM), jnp.float32),
                jnp.zeros((SEQLEN, KV_HEADS * HEAD_DIM), jnp.float32),
                jnp.zeros((HEADS, HEAD_DIM), jnp.float32))
        (key_acc, value_acc, gain_acc), dq_blocks = lax.scan(step, init, jnp.arange(N_SEQ, dtype=jnp.int32))
        grad_q = dq_blocks.reshape(SEQLEN, HEADS * HEAD_DIM)
        return grad_q, key_acc.astype(jnp.bfloat16), value_acc.astype(jnp.bfloat16), gain_acc

    grad_q, grad_k, grad_v, gains = lax.map(one_sequence, (queries, keys, values, grad_out, doc_ids, partner_bits))
    return grad_q, grad_k, grad_v, jnp.sum(gains, axis=0)
```

```python
import math

import jax
import jax.numpy as jnp
from jax import lax
from jax.experimental import pallas as pl
from jax.experimental.pallas import tpu as pltpu
from jax.sharding import PartitionSpec as P

HIDDEN = -1e30


def passed_along(value, axis, steps):
    count = lax.axis_size(axis)
    leading, last = (max(0, -steps), min(count, count - steps))
    return lax.ppermute(value, axis, [(source, source + steps) for source in range(leading, last)])


def summed(value, axis):
    count = lax.axis_size(axis)
    copies = jnp.broadcast_to(value[None], (count,) + value.shape)
    return jnp.sum(lax.all_to_all(copies, axis, 0, 0, tiled=True), axis=0)


def attention_kernel(levels, kv_heads, group, blk, hdim, *refs):
    here_ref, bits_ref, docs_ref, q_ref, g_ref, gain_ref, k_ref, v_ref = refs[:8]
    far_refs = refs[8 : 8 + levels]
    dq_ref, own_ref = refs[8 + levels : 10 + levels]
    term_refs = refs[10 + levels : 10 + 2 * levels]
    gg_ref = refs[10 + 2 * levels]
    bias_s, s_s, dp_s, ph_s, ds_s = refs[11 + 2 * levels :]
    scale = hdim ** (-0.5)
    here = here_ref[0]
    bits = bits_ref[0, here]
    width = group * hdim
    kv_width = kv_heads * hdim

    def doc_row(block):
        return docs_ref[0:1, pl.ds(pl.multiple_of(block * blk, blk), blk)]

    q_docs = doc_row(here)
    for level in range(levels + 1):
        dist = 0 if level == 0 else 2 ** (level - 1)
        k_docs = jnp.broadcast_to(doc_row(jnp.maximum(here - dist, 0)), (blk, blk)).T
        seen = k_docs == q_docs
        if level == 0:
            key_pos = lax.broadcasted_iota(jnp.int32, (blk, blk), 0)
            query_pos = lax.broadcasted_iota(jnp.int32, (blk, blk), 1)
            seen = seen & (key_pos <= query_pos)
            bias = jnp.where(seen, 0.0, HIDDEN)
        else:
            live = (((bits >> (level - 1)) & 1) == 1) & (here >= dist)
            bias = jnp.where(seen, jnp.where(live, 0.0, HIDDEN), HIDDEN)
        bias_s[level * blk : (level + 1) * blk, :] = bias.astype(jnp.float32)

    for head in range(kv_heads):
        lo, klo = head * width, head * hdim
        q_parts, g_parts = [], []
        for i in range(group):
            one = q_ref[0, :, lo + i * hdim : lo + (i + 1) * hdim].astype(jnp.float32)
            gain = gain_ref[head * group + i : head * group + i + 1, :]
            q_parts.append((one * gain).astype(jnp.bfloat16))
            g_parts.append(g_ref[0, :, lo + i * hdim : lo + (i + 1) * hdim])
        q_cat = jnp.concatenate(q_parts, 0)
        g_cat = jnp.concatenate(g_parts, 0)
        k_all = jnp.concatenate(
            [k_ref[0, :, klo : klo + hdim]] + [r[:, klo : klo + hdim] for r in far_refs], 0
        )
        v_all = jnp.concatenate(
            [v_ref[0, :, klo : klo + hdim]]
            + [r[:, kv_width + klo : kv_width + klo + hdim] for r in far_refs],
            0,
        )
        across = (((1,), (1,)), ((), ()))
        s_s[...] = lax.dot_general(k_all, q_cat, across, preferred_element_type=jnp.float32)
        dp_s[...] = lax.dot_general(v_all, g_cat, across, preferred_element_type=jnp.float32)
        top = None
        for level in range(levels + 1):
            rows = slice(level * blk, (level + 1) * blk)
            bias = bias_s[rows, :]
            s = s_s[rows, :] + jnp.concatenate([bias] * group, 1)
            s_s[rows, :] = s
            part = jnp.max(s, axis=0, keepdims=True)
            top = part if top is None else jnp.maximum(top, part)
        total = jnp.zeros_like(top)
        weighted = jnp.zeros_like(top)
        for level in range(levels + 1):
            rows = slice(level * blk, (level + 1) * blk)
            p = jnp.exp2((s_s[rows, :] - top) * jnp.float32(scale * math.log2(math.e)))
            s_s[rows, :] = p
            total = total + jnp.sum(p, axis=0, keepdims=True)
            weighted = weighted + jnp.sum(p * dp_s[rows, :], axis=0, keepdims=True)
        inverse = 1.0 / total
        delta = weighted * inverse
        for level in range(levels + 1):
            rows = slice(level * blk, (level + 1) * blk)
            prob = s_s[rows, :] * inverse
            ph_s[rows, :] = prob.astype(jnp.bfloat16)
            ds_s[rows, :] = (prob * (dp_s[rows, :] - delta)).astype(jnp.bfloat16)
        ds = ds_s[...]
        dk = jnp.dot(ds, q_cat, preferred_element_type=jnp.float32) * scale
        dv = jnp.dot(ph_s[...], g_cat, preferred_element_type=jnp.float32)
        own_ref[:, klo : klo + hdim] = dk[:blk]
        own_ref[:, kv_width + klo : kv_width + klo + hdim] = dv[:blk]
        for level in range(levels):
            rows = slice((level + 1) * blk, (level + 2) * blk)
            term_refs[level][:, klo : klo + hdim] = dk[rows].astype(jnp.bfloat16)
            term_refs[level][:, kv_width + klo : kv_width + klo + hdim] = dv[rows].astype(
                jnp.bfloat16
            )
        dq_t = (
            lax.dot_general(
                k_all, ds, (((0,), (0,)), ((), ())), preferred_element_type=jnp.float32
            )
            * scale
        )
        for i in range(group):
            cols = slice(lo + i * hdim, lo + (i + 1) * hdim)
            row = slice(head * group + i, head * group + i + 1)
            dq = dq_t[:, i * blk : (i + 1) * blk].T
            raw = q_ref[0, :, cols].astype(jnp.float32)
            gg_ref[row, :] = jnp.sum(dq * raw, axis=0, keepdims=True)
            dq_ref[0, :, cols] = (dq * gain_ref[row, :]).astype(jnp.bfloat16)


def attention(here, bits, docs, queries, grad_out, q_gain, keys, values, far):
    levels = len(far)
    blk = queries.shape[1]
    heads, hdim = q_gain.shape
    kv_width = keys.shape[2]
    kv_heads = kv_width // hdim
    group = heads // kv_heads
    all_rows = (levels + 1) * blk
    vmem = pl.BlockSpec(memory_space=pltpu.VMEM)
    smem = pl.BlockSpec(memory_space=pltpu.SMEM)

    def kernel(*refs):
        attention_kernel(levels, kv_heads, group, blk, hdim, *refs)

    return pl.pallas_call(
        kernel,
        out_shape=[
            jax.ShapeDtypeStruct(queries.shape, jnp.bfloat16),
            jax.ShapeDtypeStruct((blk, 2 * kv_width), jnp.float32),
        ]
        + [jax.ShapeDtypeStruct((blk, 2 * kv_width), jnp.bfloat16)] * levels
        + [jax.ShapeDtypeStruct((heads, hdim), jnp.float32)],
        in_specs=[smem, smem] + [vmem] * (6 + levels),
        out_specs=[vmem] * (3 + levels),
        scratch_shapes=[
            pltpu.VMEM((all_rows, blk), jnp.float32),
            pltpu.VMEM((all_rows, group * blk), jnp.float32),
            pltpu.VMEM((all_rows, group * blk), jnp.float32),
            pltpu.VMEM((all_rows, group * blk), jnp.bfloat16),
            pltpu.VMEM((all_rows, group * blk), jnp.bfloat16),
        ],
        compiler_params=pltpu.CompilerParams(vmem_limit_bytes=40 * 2**20),
        name="attention_both_ways",
    )(here, bits, docs, queries, grad_out, q_gain, keys, values, *far)


def local(queries, keys, values, grad_out, doc_ids, partner_bits, q_gain):
    count = lax.axis_size("seq")
    levels = count.bit_length() - 1
    here = lax.axis_index("seq")
    kv_width = keys.shape[2]
    own = jnp.concatenate([keys[0], values[0]], 1)
    far = [passed_along(own, "seq", 2**level) for level in range(levels)]
    results = attention(
        here.astype(jnp.int32)[None],
        partner_bits,
        doc_ids,
        queries,
        grad_out,
        q_gain,
        keys,
        values,
        far,
    )
    grad_q, total, terms, gain_term = results[0], results[1], results[2:-1], results[-1]
    for level in range(levels):
        total = total + passed_along(terms[level], "seq", -(2**level)).astype(jnp.float32)
    grad_gain = summed(summed(gain_term, "seq"), "dp")
    return (
        grad_q,
        total[:, :kv_width].astype(jnp.bfloat16)[None],
        total[:, kv_width:].astype(jnp.bfloat16)[None],
        grad_gain,
    )


def solution(mesh):
    return jax.shard_map(
        local,
        mesh=mesh,
        in_specs=(
            P("dp", "seq", None),
            P("dp", "seq", None),
            P("dp", "seq", None),
            P("dp", "seq", None),
            P("dp", None),
            P("dp", None),
            P(),
        ),
        out_specs=(P("dp", "seq", None), P("dp", "seq", None), P("dp", "seq", None), P()),
        check_vma=False,
    )
```

```python
import math

import jax
import jax.numpy as jnp
from jax import lax
from jax.experimental import pallas as pl
from jax.experimental.pallas import tpu as pltpu
from jax.sharding import PartitionSpec as P

HIDDEN = -1e30
ROW = 4
ACROSS = (((1,), (1,)), ((), ()))
VMEM = pl.BlockSpec(memory_space=pltpu.VMEM)
SMEM = pl.BlockSpec(memory_space=pltpu.SMEM)


def passed_along(value, steps):
    count = lax.axis_size("seq")
    leading, last = (max(0, -steps), min(count, count - steps))
    return lax.ppermute(value, "seq", [(source, source + steps) for source in range(leading, last)])


def passed_in_row(value, steps):
    count = lax.axis_size("seq")
    pairs = [(b, b // ROW * ROW + (b + steps) % ROW) for b in range(count)]
    return lax.ppermute(value, "seq", pairs)


def passed_between_rows(value, row, rows, step):
    count = lax.axis_size("seq")

    def branch(first):
        pairs = [
            (first * ROW + x, (first + step) * ROW + x)
            for x in range(ROW)
            if 0 <= (first + step) * ROW < count
        ]
        return lambda block: lax.ppermute(block, "seq", pairs)

    return lax.switch(row, [jnp.zeros_like] + [branch(first) for first in rows], value)


def summed(value, axis):
    count = lax.axis_size(axis)
    copies = jnp.broadcast_to(value[None], (count,) + value.shape)
    return jnp.sum(lax.all_to_all(copies, axis, 0, 0, tiled=True), axis=0)


def prepare_kernel(levels, kv_heads, group, blk, hdim, *refs):
    here_ref, bits_ref, docs_ref, q_ref, g_ref, gain_ref, own_ref = refs[:7]
    bias_ref, q_out, g_out, s_ref, dp_ref = refs[7:]
    here = here_ref[0]
    bits = bits_ref[0, here]
    kv_width = kv_heads * hdim

    for head in range(kv_heads):
        base = head * group * blk
        for i in range(group):
            cols = slice((head * group + i) * hdim, (head * group + i + 1) * hdim)
            rows = slice(base + i * blk, base + (i + 1) * blk)
            gain = gain_ref[head * group + i : head * group + i + 1, :]
            q_out[rows, :] = (q_ref[0, :, cols].astype(jnp.float32) * gain).astype(jnp.bfloat16)
            g_out[rows, :] = g_ref[0, :, cols]
        rows = slice(base, base + group * blk)
        out = slice(head * blk, (head + 1) * blk)
        k_own = own_ref[:, head * hdim : (head + 1) * hdim]
        v_own = own_ref[:, kv_width + head * hdim : kv_width + (head + 1) * hdim]
        s_ref[out, :] = lax.dot_general(
            k_own, q_out[rows, :], ACROSS, preferred_element_type=jnp.float32
        )
        dp_ref[out, :] = lax.dot_general(
            v_own, g_out[rows, :], ACROSS, preferred_element_type=jnp.float32
        )

    def doc_row(block):
        return docs_ref[0:1, pl.ds(pl.multiple_of(block * blk, blk), blk)]

    q_docs = doc_row(here)
    for level in range(levels + 1):
        dist = 0 if level == 0 else 2 ** (level - 1)
        k_docs = jnp.broadcast_to(doc_row(jnp.maximum(here - dist, 0)), (blk, blk)).T
        seen = k_docs == q_docs
        if level == 0:
            key_pos = lax.broadcasted_iota(jnp.int32, (blk, blk), 0)
            query_pos = lax.broadcasted_iota(jnp.int32, (blk, blk), 1)
            bias = jnp.where(seen & (key_pos <= query_pos), 0.0, HIDDEN)
        else:
            live = (((bits >> (level - 1)) & 1) == 1) & (here >= dist)
            bias = jnp.where(seen, jnp.where(live, 0.0, HIDDEN), HIDDEN)
        bias_ref[level * blk : (level + 1) * blk, :] = bias.astype(jnp.float32)


def attention_kernel(levels, kv_heads, group, blk, hdim, *refs):
    q_ref, gain_ref, bias_ref, qc_ref, gc_ref, s_ref, dp_ref, own_ref = refs[:8]
    far_refs = refs[8 : 8 + levels]
    dq_ref, sum_ref = refs[8 + levels : 10 + levels]
    term_refs = refs[10 + levels : 10 + 2 * levels]
    gg_ref = refs[10 + 2 * levels]
    s_s, dp_s, ph_s, ds_s = refs[11 + 2 * levels :]
    scale = hdim ** (-0.5)
    width = group * hdim
    kv_width = kv_heads * hdim

    for head in range(kv_heads):
        lo, klo = head * width, head * hdim
        kcols = slice(klo, klo + hdim)
        vcols = slice(kv_width + klo, kv_width + klo + hdim)
        q_cat = qc_ref[head * group * blk : (head + 1) * group * blk, :]
        g_cat = gc_ref[head * group * blk : (head + 1) * group * blk, :]
        k_far = jnp.concatenate([r[:, kcols] for r in far_refs], 0)
        v_far = jnp.concatenate([r[:, vcols] for r in far_refs], 0)
        s_s[blk:, :] = lax.dot_general(k_far, q_cat, ACROSS, preferred_element_type=jnp.float32)
        dp_s[blk:, :] = lax.dot_general(v_far, g_cat, ACROSS, preferred_element_type=jnp.float32)
        here = slice(head * blk, (head + 1) * blk)
        top = None
        for level in range(levels + 1):
            rows = slice(level * blk, (level + 1) * blk)
            s = s_ref[here, :] if level == 0 else s_s[rows, :]
            s = s + jnp.concatenate([bias_ref[rows, :]] * group, 1)
            s_s[rows, :] = s
            part = jnp.max(s, axis=0, keepdims=True)
            top = part if top is None else jnp.maximum(top, part)
        total = jnp.zeros_like(top)
        weighted = jnp.zeros_like(top)
        for level in range(levels + 1):
            rows = slice(level * blk, (level + 1) * blk)
            p = jnp.exp2((s_s[rows, :] - top) * jnp.float32(scale * math.log2(math.e)))
            s_s[rows, :] = p
            dp = dp_ref[here, :] if level == 0 else dp_s[rows, :]
            total = total + jnp.sum(p, axis=0, keepdims=True)
            weighted = weighted + jnp.sum(p * dp, axis=0, keepdims=True)
        inverse = 1.0 / total
        delta = weighted * inverse
        for level in range(levels + 1):
            rows = slice(level * blk, (level + 1) * blk)
            prob = s_s[rows, :] * inverse
            ph_s[rows, :] = prob.astype(jnp.bfloat16)
            dp = dp_ref[here, :] if level == 0 else dp_s[rows, :]
            ds_s[rows, :] = (prob * (dp - delta)).astype(jnp.bfloat16)
        ds = ds_s[...]
        dk = jnp.dot(ds, q_cat, preferred_element_type=jnp.float32) * scale
        dv = jnp.dot(ph_s[...], g_cat, preferred_element_type=jnp.float32)
        sum_ref[:, kcols] = dk[:blk]
        sum_ref[:, vcols] = dv[:blk]
        for level in range(levels):
            rows = slice((level + 1) * blk, (level + 2) * blk)
            term_refs[level][:, kcols] = dk[rows].astype(jnp.bfloat16)
            term_refs[level][:, vcols] = dv[rows].astype(jnp.bfloat16)
        k_all = jnp.concatenate([own_ref[:, kcols], k_far], 0)
        dq_t = (
            lax.dot_general(
                k_all, ds, (((0,), (0,)), ((), ())), preferred_element_type=jnp.float32
            )
            * scale
        )
        for i in range(group):
            cols = slice(lo + i * hdim, lo + (i + 1) * hdim)
            row = slice(head * group + i, head * group + i + 1)
            dq = dq_t[:, i * blk : (i + 1) * blk].T
            raw = q_ref[0, :, cols].astype(jnp.float32)
            gg_ref[row, :] = jnp.sum(dq * raw, axis=0, keepdims=True)
            dq_ref[0, :, cols] = (dq * gain_ref[row, :]).astype(jnp.bfloat16)


def local(queries, keys, values, grad_out, doc_ids, partner_bits, q_gain):
    f32, bf16 = jnp.float32, jnp.bfloat16
    count = lax.axis_size("seq")
    levels = count.bit_length() - 1
    here = lax.axis_index("seq").astype(jnp.int32)
    column = here % ROW
    blk = queries.shape[1]
    heads, hdim = q_gain.shape
    kv_width = keys.shape[2]
    kv_heads = kv_width // hdim
    group = heads // kv_heads
    sizes = (levels, kv_heads, group, blk, hdim)
    all_rows = (levels + 1) * blk

    def shape(rows, columns, dtype):
        return jax.ShapeDtypeStruct((rows, columns), dtype)

    half = count // 2 // ROW
    by_block = doc_ids[0].reshape(count, blk)
    shared = by_block[: count // 2, blk - 1] == by_block[count // 2 :, 0]
    wanted = (partner_bits[0, count // 2 :] >> (levels - 1)) & 1 == 1
    far_rows = jnp.arange(count // 2, dtype=jnp.int32) // ROW + 1
    far_row = jnp.max(jnp.where(shared & wanted, far_rows, 0))

    own = jnp.concatenate([keys[0], values[0]], 1)
    by4 = passed_along(own, 4)
    by8 = passed_along(own, 8)
    by2 = passed_along(own, 2)
    by1 = passed_in_row(jnp.where(column >= ROW - 1, by4, own), 1)
    by16 = passed_between_rows(own, far_row, range(half), half)
    far = [by1, by2, by4, by8, by16]

    bias, q_cat, g_cat, s_own, dp_own = pl.pallas_call(
        lambda *refs: prepare_kernel(*sizes, *refs),
        out_shape=[
            shape(all_rows, blk, f32),
            shape(heads * blk, hdim, bf16),
            shape(heads * blk, hdim, bf16),
            shape(kv_heads * blk, group * blk, f32),
            shape(kv_heads * blk, group * blk, f32),
        ],
        in_specs=[SMEM, SMEM] + [VMEM] * 5,
        out_specs=[VMEM] * 5,
        compiler_params=pltpu.CompilerParams(vmem_limit_bytes=40 * 2**20),
        cost_estimate=pl.CostEstimate(flops=10**9, bytes_accessed=4 * 10**6, transcendentals=0),
        name="prepare",
    )(here[None], partner_bits, doc_ids, queries, grad_out, q_gain, own)

    results = pl.pallas_call(
        lambda *refs: attention_kernel(*sizes, *refs),
        out_shape=[
            jax.ShapeDtypeStruct(queries.shape, bf16),
            shape(blk, 2 * kv_width, f32),
        ]
        + [shape(blk, 2 * kv_width, bf16)] * levels
        + [shape(heads, hdim, f32)],
        in_specs=[VMEM] * (8 + levels),
        out_specs=[VMEM] * (3 + levels),
        scratch_shapes=[
            pltpu.VMEM((all_rows, group * blk), f32),
            pltpu.VMEM((all_rows, group * blk), f32),
            pltpu.VMEM((all_rows, group * blk), bf16),
            pltpu.VMEM((all_rows, group * blk), bf16),
        ],
        compiler_params=pltpu.CompilerParams(vmem_limit_bytes=40 * 2**20),
        cost_estimate=pl.CostEstimate(
            flops=2 * 10**9, bytes_accessed=6 * 10**6, transcendentals=10**6
        ),
        name="attention_both_ways",
    )(queries, q_gain, bias, q_cat, g_cat, s_own, dp_own, own, *far)
    grad_q, total, terms, gain_term = results[0], results[1], results[2:-1], results[-1]

    back = [passed_along(terms[level], -(2**level)) for level in range(levels - 1)]
    copies = jnp.broadcast_to(gain_term[None], (count,) + gain_term.shape)
    gain_term = jnp.sum(lax.all_to_all(copies, "seq", 0, 0, tiled=True), axis=0)
    gain_term, far_term = lax.optimization_barrier((gain_term, terms[-1]))
    back.append(passed_between_rows(far_term, far_row, range(half, 2 * half), -half))
    for block in back:
        total = total + block.astype(f32)
    grad_gain = summed(gain_term, "dp")
    return (
        grad_q,
        total[:, :kv_width].astype(bf16)[None],
        total[:, kv_width:].astype(bf16)[None],
        grad_gain,
    )


def solution(mesh):
    return jax.shard_map(
        local,
        mesh=mesh,
        in_specs=(
            P("dp", "seq", None),
            P("dp", "seq", None),
            P("dp", "seq", None),
            P("dp", "seq", None),
            P("dp", None),
            P("dp", None),
            P(),
        ),
        out_specs=(P("dp", "seq", None), P("dp", "seq", None), P("dp", "seq", None), P()),
        check_vma=False,
    )
```

```python
import math

import jax
import jax.numpy as jnp
from jax import lax
from jax.experimental import pallas as pl
from jax.experimental.pallas import tpu as pltpu
from jax.sharding import PartitionSpec as P

HIDDEN = -1e30
ROW = 4
ACROSS = (((1,), (1,)), ((), ()))
VMEM = pl.BlockSpec(memory_space=pltpu.VMEM)
SMEM = pl.BlockSpec(memory_space=pltpu.SMEM)


def passed_along(value, steps):
    count = lax.axis_size("seq")
    leading, last = (max(0, -steps), min(count, count - steps))
    return lax.ppermute(value, "seq", [(source, source + steps) for source in range(leading, last)])


def passed_in_row(value, steps):
    count = lax.axis_size("seq")
    pairs = [(b, b // ROW * ROW + (b + steps) % ROW) for b in range(count)]
    return lax.ppermute(value, "seq", pairs)


def passed_between_rows(value, row, rows, step):
    count = lax.axis_size("seq")

    def branch(first):
        pairs = [
            (first * ROW + x, (first + step) * ROW + x)
            for x in range(ROW)
            if 0 <= (first + step) * ROW < count
        ]
        return lambda block: lax.ppermute(block, "seq", pairs)

    return lax.switch(row, [jnp.zeros_like] + [branch(first) for first in rows], value)


def summed(value, axis):
    count = lax.axis_size(axis)
    copies = jnp.broadcast_to(value[None], (count,) + value.shape)
    return jnp.sum(lax.all_to_all(copies, axis, 0, 0, tiled=True), axis=0)


def prepare_kernel(levels, kv_heads, group, blk, hdim, *refs):
    here_ref, bits_ref, docs_ref, q_ref, g_ref, gain_ref, own_ref = refs[:7]
    bias_ref, q_out, g_out, s_ref, dp_ref = refs[7:]
    here = here_ref[0]
    bits = bits_ref[0, here]

    for head in range(kv_heads):
        base = head * group * blk
        for i in range(group):
            cols = slice((head * group + i) * hdim, (head * group + i + 1) * hdim)
            rows = slice(base + i * blk, base + (i + 1) * blk)
            gain = gain_ref[head * group + i : head * group + i + 1, :]
            q_out[rows, :] = (q_ref[0, :, cols].astype(jnp.float32) * gain).astype(jnp.bfloat16)
            g_out[rows, :] = g_ref[0, :, cols]
        rows = slice(base, base + group * blk)
        out = slice(head * blk, (head + 1) * blk)
        k_own = own_ref[0, :, head * hdim : (head + 1) * hdim]
        v_own = own_ref[1, :, head * hdim : (head + 1) * hdim]
        s_ref[out, :] = lax.dot_general(
            k_own, q_out[rows, :], ACROSS, preferred_element_type=jnp.float32
        )
        dp_ref[out, :] = lax.dot_general(
            v_own, g_out[rows, :], ACROSS, preferred_element_type=jnp.float32
        )

    def doc_row(block):
        return docs_ref[0:1, pl.ds(pl.multiple_of(block * blk, blk), blk)]

    q_docs = doc_row(here)
    for level in range(levels + 1):
        dist = 0 if level == 0 else 2 ** (level - 1)
        k_docs = jnp.broadcast_to(doc_row(jnp.maximum(here - dist, 0)), (blk, blk)).T
        seen = k_docs == q_docs
        if level == 0:
            key_pos = lax.broadcasted_iota(jnp.int32, (blk, blk), 0)
            query_pos = lax.broadcasted_iota(jnp.int32, (blk, blk), 1)
            bias = jnp.where(seen & (key_pos <= query_pos), 0.0, HIDDEN)
        else:
            live = (((bits >> (level - 1)) & 1) == 1) & (here >= dist)
            bias = jnp.where(seen, jnp.where(live, 0.0, HIDDEN), HIDDEN)
        bias_ref[level * blk : (level + 1) * blk, :] = bias.astype(jnp.float32)


def attention_kernel(levels, kv_heads, group, blk, hdim, *refs):
    q_ref, gain_ref, bias_ref, qc_ref, gc_ref, s_ref, dp_ref, own_ref = refs[:8]
    far_refs = refs[8 : 8 + levels]
    dq_ref, sum_ref = refs[8 + levels : 10 + levels]
    term_refs = refs[10 + levels : 10 + 2 * levels]
    gg_ref = refs[10 + 2 * levels]
    s_s, dp_s, ph_s, ds_s, last_ref, sem = refs[11 + 2 * levels :]
    near_refs = far_refs[:-1]
    last = levels * blk
    copy = pltpu.make_async_copy(far_refs[-1], last_ref, sem)
    copy.start()
    scale = hdim ** (-0.5)
    width = group * hdim

    for head in range(kv_heads):
        lo, klo = head * width, head * hdim
        kcols = slice(klo, klo + hdim)
        q_cat = qc_ref[head * group * blk : (head + 1) * group * blk, :]
        g_cat = gc_ref[head * group * blk : (head + 1) * group * blk, :]
        k_near = jnp.concatenate([r[0, :, kcols] for r in near_refs], 0)
        v_near = jnp.concatenate([r[1, :, kcols] for r in near_refs], 0)
        s_s[blk:last, :] = lax.dot_general(
            k_near, q_cat, ACROSS, preferred_element_type=jnp.float32
        )
        dp_s[blk:last, :] = lax.dot_general(
            v_near, g_cat, ACROSS, preferred_element_type=jnp.float32
        )
        if head == 0:
            copy.wait()
        k_last = last_ref[0, :, kcols]
        s_s[last:, :] = lax.dot_general(
            k_last, q_cat, ACROSS, preferred_element_type=jnp.float32
        )
        dp_s[last:, :] = lax.dot_general(
            last_ref[1, :, kcols], g_cat, ACROSS, preferred_element_type=jnp.float32
        )
        here = slice(head * blk, (head + 1) * blk)
        top = None
        for level in range(levels + 1):
            rows = slice(level * blk, (level + 1) * blk)
            s = s_ref[here, :] if level == 0 else s_s[rows, :]
            s = s + jnp.concatenate([bias_ref[rows, :]] * group, 1)
            s_s[rows, :] = s
            part = jnp.max(s, axis=0, keepdims=True)
            top = part if top is None else jnp.maximum(top, part)
        total = jnp.zeros_like(top)
        weighted = jnp.zeros_like(top)
        for level in range(levels + 1):
            rows = slice(level * blk, (level + 1) * blk)
            p = jnp.exp2((s_s[rows, :] - top) * jnp.float32(scale * math.log2(math.e)))
            s_s[rows, :] = p
            dp = dp_ref[here, :] if level == 0 else dp_s[rows, :]
            total = total + jnp.sum(p, axis=0, keepdims=True)
            weighted = weighted + jnp.sum(p * dp, axis=0, keepdims=True)
        inverse = 1.0 / total
        delta = weighted * inverse
        for level in range(levels + 1):
            rows = slice(level * blk, (level + 1) * blk)
            prob = s_s[rows, :] * inverse
            ph_s[rows, :] = prob.astype(jnp.bfloat16)
            dp = dp_ref[here, :] if level == 0 else dp_s[rows, :]
            ds_s[rows, :] = (prob * (dp - delta)).astype(jnp.bfloat16)
        ds = ds_s[...]
        dk = jnp.dot(ds, q_cat, preferred_element_type=jnp.float32) * scale
        dv = jnp.dot(ph_s[...], g_cat, preferred_element_type=jnp.float32)
        sum_ref[0, :, kcols] = dk[:blk]
        sum_ref[1, :, kcols] = dv[:blk]
        for level in range(levels):
            rows = slice((level + 1) * blk, (level + 2) * blk)
            term_refs[level][0, :, kcols] = dk[rows].astype(jnp.bfloat16)
            term_refs[level][1, :, kcols] = dv[rows].astype(jnp.bfloat16)
        k_all = jnp.concatenate([own_ref[0, :, kcols], k_near, k_last], 0)
        dq_t = (
            lax.dot_general(
                k_all, ds, (((0,), (0,)), ((), ())), preferred_element_type=jnp.float32
            )
            * scale
        )
        for i in range(group):
            cols = slice(lo + i * hdim, lo + (i + 1) * hdim)
            row = slice(head * group + i, head * group + i + 1)
            dq = dq_t[:, i * blk : (i + 1) * blk].T
            raw = q_ref[0, :, cols].astype(jnp.float32)
            gg_ref[row, :] = jnp.sum(dq * raw, axis=0, keepdims=True)
            dq_ref[0, :, cols] = (dq * gain_ref[row, :]).astype(jnp.bfloat16)


def local(queries, keys, values, grad_out, doc_ids, partner_bits, q_gain):
    f32, bf16 = jnp.float32, jnp.bfloat16
    count = lax.axis_size("seq")
    levels = count.bit_length() - 1
    here = lax.axis_index("seq").astype(jnp.int32)
    column = here % ROW
    blk = queries.shape[1]
    heads, hdim = q_gain.shape
    kv_width = keys.shape[2]
    kv_heads = kv_width // hdim
    group = heads // kv_heads
    sizes = (levels, kv_heads, group, blk, hdim)
    all_rows = (levels + 1) * blk

    def shape(rows, columns, dtype):
        return jax.ShapeDtypeStruct((rows, columns), dtype)

    half = count // 2 // ROW
    by_block = doc_ids[0].reshape(count, blk)
    shared = by_block[: count // 2, blk - 1] == by_block[count // 2 :, 0]
    wanted = (partner_bits[0, count // 2 :] >> (levels - 1)) & 1 == 1
    far_rows = jnp.arange(count // 2, dtype=jnp.int32) // ROW + 1
    far_row = jnp.max(jnp.where(shared & wanted, far_rows, 0))

    own = jnp.stack([keys[0], values[0]])
    by4 = passed_along(own, 4)
    by8 = passed_along(own, 8)
    by2 = passed_along(own, 2)
    by1 = passed_in_row(jnp.where(column >= ROW - 1, by4, own), 1)
    by16 = passed_between_rows(own, far_row, range(half), half)
    far = [by1, by2, by4, by8, by16]

    bias, q_cat, g_cat, s_own, dp_own = pl.pallas_call(
        lambda *refs: prepare_kernel(*sizes, *refs),
        out_shape=[
            shape(all_rows, blk, f32),
            shape(heads * blk, hdim, bf16),
            shape(heads * blk, hdim, bf16),
            shape(kv_heads * blk, group * blk, f32),
            shape(kv_heads * blk, group * blk, f32),
        ],
        in_specs=[SMEM, SMEM] + [VMEM] * 5,
        out_specs=[VMEM] * 5,
        compiler_params=pltpu.CompilerParams(vmem_limit_bytes=40 * 2**20),
        cost_estimate=pl.CostEstimate(flops=10**9, bytes_accessed=4 * 10**6, transcendentals=0),
        name="prepare",
    )(here[None], partner_bits, doc_ids, queries, grad_out, q_gain, own)

    results = pl.pallas_call(
        lambda *refs: attention_kernel(*sizes, *refs),
        out_shape=[
            jax.ShapeDtypeStruct(queries.shape, bf16),
            jax.ShapeDtypeStruct((2, blk, kv_width), f32),
        ]
        + [jax.ShapeDtypeStruct((2, blk, kv_width), bf16)] * levels
        + [shape(heads, hdim, f32)],
        in_specs=[VMEM] * (7 + levels) + [pl.BlockSpec(memory_space=pl.ANY)],
        out_specs=[VMEM] * (3 + levels),
        scratch_shapes=[
            pltpu.VMEM((all_rows, group * blk), f32),
            pltpu.VMEM((all_rows, group * blk), f32),
            pltpu.VMEM((all_rows, group * blk), bf16),
            pltpu.VMEM((all_rows, group * blk), bf16),
            pltpu.VMEM((2, blk, kv_width), bf16),
            pltpu.SemaphoreType.DMA,
        ],
        compiler_params=pltpu.CompilerParams(vmem_limit_bytes=40 * 2**20),
        cost_estimate=pl.CostEstimate(
            flops=2 * 10**9, bytes_accessed=6 * 10**6, transcendentals=10**6
        ),
        name="attention_both_ways",
    )(queries, q_gain, bias, q_cat, g_cat, s_own, dp_own, own, *far)
    grad_q, total, terms, gain_term = results[0], results[1], results[2:-1], results[-1]

    back = [passed_along(terms[level], -(2**level)) for level in range(levels - 1)]
    copies = jnp.broadcast_to(gain_term[None], (count,) + gain_term.shape)
    gain_term = jnp.sum(lax.all_to_all(copies, "seq", 0, 0, tiled=True), axis=0)
    gain_term, far_term = lax.optimization_barrier((gain_term, terms[-1]))
    back16 = passed_between_rows(far_term, far_row, range(half, 2 * half), -half)
    back.append(jnp.where(far_row > 0, back16, 0))
    for block in back:
        total = total + block.astype(f32)
    grad_gain = summed(gain_term, "dp")
    return (
        grad_q,
        total[:1].astype(bf16),
        total[1:].astype(bf16),
        grad_gain,
    )


def solution(mesh):
    return jax.shard_map(
        local,
        mesh=mesh,
        in_specs=(
            P("dp", "seq", None),
            P("dp", "seq", None),
            P("dp", "seq", None),
            P("dp", "seq", None),
            P("dp", None),
            P("dp", None),
            P(),
        ),
        out_specs=(P("dp", "seq", None), P("dp", "seq", None), P("dp", "seq", None), P()),
        check_vma=False,
    )
```

```python
import math

import jax
import jax.numpy as jnp
from jax import lax
from jax.experimental import pallas as pl
from jax.experimental.pallas import tpu as pltpu
from jax.sharding import PartitionSpec as P

HIDDEN = -1e30
ROW = 4
ACROSS = (((1,), (1,)), ((), ()))
VMEM = pl.BlockSpec(memory_space=pltpu.VMEM)
SMEM = pl.BlockSpec(memory_space=pltpu.SMEM)


def passed_along(value, steps):
    count = lax.axis_size("seq")
    leading, last = (max(0, -steps), min(count, count - steps))
    return lax.ppermute(value, "seq", [(source, source + steps) for source in range(leading, last)])


def passed_in_row(value, steps):
    count = lax.axis_size("seq")
    pairs = [(b, b // ROW * ROW + (b + steps) % ROW) for b in range(count)]
    return lax.ppermute(value, "seq", pairs)


def passed_between_rows(value, row, rows, step):
    count = lax.axis_size("seq")

    def branch(first):
        pairs = [
            (first * ROW + x, (first + step) * ROW + x)
            for x in range(ROW)
            if 0 <= (first + step) * ROW < count
        ]
        return lambda block: lax.ppermute(block, "seq", pairs)

    return lax.switch(row, [jnp.zeros_like] + [branch(first) for first in rows], value)


def summed(value, axis):
    count = lax.axis_size(axis)
    copies = jnp.broadcast_to(value[None], (count,) + value.shape)
    return jnp.sum(lax.all_to_all(copies, axis, 0, 0, tiled=True), axis=0)


def prepare_kernel(levels, kv_heads, group, blk, hdim, *refs):
    here_ref, bits_ref, docs_ref, q_ref, g_ref, gain_ref, own_ref = refs[:7]
    bias_ref, q_out, g_out, s_ref, dp_ref = refs[7:]
    here = here_ref[0]
    bits = bits_ref[0, here]

    for head in range(kv_heads):
        base = head * group * blk
        for i in range(group):
            cols = slice((head * group + i) * hdim, (head * group + i + 1) * hdim)
            rows = slice(base + i * blk, base + (i + 1) * blk)
            gain = gain_ref[head * group + i : head * group + i + 1, :]
            q_out[rows, :] = (q_ref[0, :, cols].astype(jnp.float32) * gain).astype(jnp.bfloat16)
            g_out[rows, :] = g_ref[0, :, cols]
        rows = slice(base, base + group * blk)
        out = slice(head * blk, (head + 1) * blk)
        k_own = own_ref[0, :, head * hdim : (head + 1) * hdim]
        v_own = own_ref[1, :, head * hdim : (head + 1) * hdim]
        s_ref[out, :] = lax.dot_general(
            k_own, q_out[rows, :], ACROSS, preferred_element_type=jnp.float32
        )
        dp_ref[out, :] = lax.dot_general(
            v_own, g_out[rows, :], ACROSS, preferred_element_type=jnp.float32
        )

    def doc_row(block):
        return docs_ref[0:1, pl.ds(pl.multiple_of(block * blk, blk), blk)]

    q_docs = doc_row(here)
    for level in range(levels + 1):
        dist = 0 if level == 0 else 2 ** (level - 1)
        k_docs = jnp.broadcast_to(doc_row(jnp.maximum(here - dist, 0)), (blk, blk)).T
        seen = k_docs == q_docs
        if level == 0:
            key_pos = lax.broadcasted_iota(jnp.int32, (blk, blk), 0)
            query_pos = lax.broadcasted_iota(jnp.int32, (blk, blk), 1)
            bias = jnp.where(seen & (key_pos <= query_pos), 0.0, HIDDEN)
        else:
            live = (((bits >> (level - 1)) & 1) == 1) & (here >= dist)
            bias = jnp.where(seen, jnp.where(live, 0.0, HIDDEN), HIDDEN)
        bias_ref[level * blk : (level + 1) * blk, :] = bias.astype(jnp.float32)


def attention_kernel(levels, kv_heads, group, blk, hdim, *refs):
    q_ref, gain_ref, bias_ref, qc_ref, gc_ref, s_ref, dp_ref, own_ref = refs[:8]
    far_refs = refs[8 : 8 + levels]
    dq_ref, sum_ref = refs[8 + levels : 10 + levels]
    term_refs = refs[10 + levels : 10 + 2 * levels]
    gg_ref = refs[10 + 2 * levels]
    s_s, dp_s, ph_s, ds_s, last_ref, sem = refs[11 + 2 * levels :]
    near_refs = far_refs[:-1]
    last = levels * blk
    copy = pltpu.make_async_copy(far_refs[-1], last_ref, sem)
    copy.start()
    scale = hdim ** (-0.5)
    width = group * hdim

    for head in range(kv_heads):
        lo, klo = head * width, head * hdim
        kcols = slice(klo, klo + hdim)
        q_cat = qc_ref[head * group * blk : (head + 1) * group * blk, :]
        g_cat = gc_ref[head * group * blk : (head + 1) * group * blk, :]
        k_near = jnp.concatenate([r[0, :, kcols] for r in near_refs], 0)
        v_near = jnp.concatenate([r[1, :, kcols] for r in near_refs], 0)
        s_s[blk:last, :] = lax.dot_general(
            k_near, q_cat, ACROSS, preferred_element_type=jnp.float32
        )
        dp_s[blk:last, :] = lax.dot_general(
            v_near, g_cat, ACROSS, preferred_element_type=jnp.float32
        )
        if head == 0:
            copy.wait()
        k_last = last_ref[0, :, kcols]
        s_s[last:, :] = lax.dot_general(
            k_last, q_cat, ACROSS, preferred_element_type=jnp.float32
        )
        dp_s[last:, :] = lax.dot_general(
            last_ref[1, :, kcols], g_cat, ACROSS, preferred_element_type=jnp.float32
        )
        here = slice(head * blk, (head + 1) * blk)
        top = None
        for level in range(levels + 1):
            rows = slice(level * blk, (level + 1) * blk)
            s = s_ref[here, :] if level == 0 else s_s[rows, :]
            s = s + jnp.concatenate([bias_ref[rows, :]] * group, 1)
            s_s[rows, :] = s
            part = jnp.max(s, axis=0, keepdims=True)
            top = part if top is None else jnp.maximum(top, part)
        total = jnp.zeros_like(top)
        weighted = jnp.zeros_like(top)
        for level in range(levels + 1):
            rows = slice(level * blk, (level + 1) * blk)
            p = jnp.exp2((s_s[rows, :] - top) * jnp.float32(scale * math.log2(math.e)))
            s_s[rows, :] = p
            dp = dp_ref[here, :] if level == 0 else dp_s[rows, :]
            total = total + jnp.sum(p, axis=0, keepdims=True)
            weighted = weighted + jnp.sum(p * dp, axis=0, keepdims=True)
        inverse = 1.0 / total
        delta = weighted * inverse
        for level in range(levels + 1):
            rows = slice(level * blk, (level + 1) * blk)
            prob = s_s[rows, :] * inverse
            ph_s[rows, :] = prob.astype(jnp.bfloat16)
            dp = dp_ref[here, :] if level == 0 else dp_s[rows, :]
            ds_s[rows, :] = (prob * (dp - delta)).astype(jnp.bfloat16)
        ds = ds_s[...]
        dk = jnp.dot(ds, q_cat, preferred_element_type=jnp.float32) * scale
        dv = jnp.dot(ph_s[...], g_cat, preferred_element_type=jnp.float32)
        sum_ref[0, :, kcols] = dk[:blk]
        sum_ref[1, :, kcols] = dv[:blk]
        for level in range(levels):
            rows = slice((level + 1) * blk, (level + 2) * blk)
            term_refs[level][0, :, kcols] = dk[rows].astype(jnp.bfloat16)
            term_refs[level][1, :, kcols] = dv[rows].astype(jnp.bfloat16)
        k_all = jnp.concatenate([own_ref[0, :, kcols], k_near, k_last], 0)
        dq_t = (
            lax.dot_general(
                k_all, ds, (((0,), (0,)), ((), ())), preferred_element_type=jnp.float32
            )
            * scale
        )
        for i in range(group):
            cols = slice(lo + i * hdim, lo + (i + 1) * hdim)
            row = slice(head * group + i, head * group + i + 1)
            dq = dq_t[:, i * blk : (i + 1) * blk].T
            raw = q_ref[0, :, cols].astype(jnp.float32)
            gg_ref[row, :] = jnp.sum(dq * raw, axis=0, keepdims=True)
            dq_ref[0, :, cols] = (dq * gain_ref[row, :]).astype(jnp.bfloat16)


def local(queries, keys, values, grad_out, doc_ids, partner_bits, q_gain):
    f32, bf16 = jnp.float32, jnp.bfloat16
    count = lax.axis_size("seq")
    levels = count.bit_length() - 1
    here = lax.axis_index("seq").astype(jnp.int32)
    column = here % ROW
    blk = queries.shape[1]
    heads, hdim = q_gain.shape
    kv_width = keys.shape[2]
    kv_heads = kv_width // hdim
    group = heads // kv_heads
    sizes = (levels, kv_heads, group, blk, hdim)
    all_rows = (levels + 1) * blk

    def shape(rows, columns, dtype):
        return jax.ShapeDtypeStruct((rows, columns), dtype)

    half = count // 2 // ROW
    by_block = doc_ids[0].reshape(count, blk)
    shared = by_block[: count // 2, blk - 1] == by_block[count // 2 :, 0]
    wanted = (partner_bits[0, count // 2 :] >> (levels - 1)) & 1 == 1
    far_rows = jnp.arange(count // 2, dtype=jnp.int32) // ROW + 1
    far_row = jnp.max(jnp.where(shared & wanted, far_rows, 0))

    own = jnp.stack([keys[0], values[0]])
    by4 = passed_along(own, 4)
    by8 = passed_along(own, 8)
    by2 = passed_along(own, 2)
    by1 = passed_in_row(jnp.where(column >= ROW - 1, by4, own), 1)
    by16 = passed_between_rows(own, far_row, range(half), half)
    far = [by1, by2, by4, by8, by16]

    bias, q_cat, g_cat, s_own, dp_own = pl.pallas_call(
        lambda *refs: prepare_kernel(*sizes, *refs),
        out_shape=[
            shape(all_rows, blk, f32),
            shape(heads * blk, hdim, bf16),
            shape(heads * blk, hdim, bf16),
            shape(kv_heads * blk, group * blk, f32),
            shape(kv_heads * blk, group * blk, f32),
        ],
        in_specs=[SMEM, SMEM] + [VMEM] * 5,
        out_specs=[VMEM] * 5,
        compiler_params=pltpu.CompilerParams(vmem_limit_bytes=40 * 2**20),
        cost_estimate=pl.CostEstimate(flops=10**9, bytes_accessed=4 * 10**6, transcendentals=0),
        name="prepare",
    )(here[None], partner_bits, doc_ids, queries, grad_out, q_gain, own)

    results = pl.pallas_call(
        lambda *refs: attention_kernel(*sizes, *refs),
        out_shape=[
            jax.ShapeDtypeStruct(queries.shape, bf16),
            jax.ShapeDtypeStruct((2, blk, kv_width), f32),
        ]
        + [jax.ShapeDtypeStruct((2, blk, kv_width), bf16)] * levels
        + [shape(heads, hdim, f32)],
        in_specs=[VMEM] * (7 + levels) + [pl.BlockSpec(memory_space=pl.ANY)],
        out_specs=[VMEM] * (3 + levels),
        scratch_shapes=[
            pltpu.VMEM((all_rows, group * blk), f32),
            pltpu.VMEM((all_rows, group * blk), f32),
            pltpu.VMEM((all_rows, group * blk), bf16),
            pltpu.VMEM((all_rows, group * blk), bf16),
            pltpu.VMEM((2, blk, kv_width), bf16),
            pltpu.SemaphoreType.DMA,
        ],
        compiler_params=pltpu.CompilerParams(vmem_limit_bytes=40 * 2**20),
        cost_estimate=pl.CostEstimate(
            flops=2 * 10**9, bytes_accessed=6 * 10**6, transcendentals=10**6
        ),
        name="attention_both_ways",
    )(queries, q_gain, bias, q_cat, g_cat, s_own, dp_own, own, *far)
    grad_q, total, terms, gain_term = results[0], results[1], results[2:-1], results[-1]

    back = [passed_along(terms[level], -(2**level)) for level in (3, 1, 2, 0)]
    copies = jnp.broadcast_to(gain_term[None], (count,) + gain_term.shape)
    gain_term = jnp.sum(lax.all_to_all(copies, "seq", 0, 0, tiled=True), axis=0)
    gain_term, far_term = lax.optimization_barrier((gain_term, terms[-1]))
    back16 = passed_between_rows(far_term, far_row, range(half, 2 * half), -half)
    back.append(jnp.where(far_row > 0, back16, 0))
    for block in back:
        total = total + block.astype(f32)
    grad_gain = summed(gain_term, "dp")
    return (
        grad_q,
        total[:1].astype(bf16),
        total[1:].astype(bf16),
        grad_gain,
    )


def solution(mesh):
    return jax.shard_map(
        local,
        mesh=mesh,
        in_specs=(
            P("dp", "seq", None),
            P("dp", "seq", None),
            P("dp", "seq", None),
            P("dp", "seq", None),
            P("dp", None),
            P("dp", None),
            P(),
        ),
        out_specs=(P("dp", "seq", None), P("dp", "seq", None), P("dp", "seq", None), P()),
        check_vma=False,
    )
```
